32 devices in a mesh: dp: 4 (over z), blk: 2 (over y), ulysses: 4 (over x, core).
Axes of the slice: x: 2, y: 2, z: 4, core: 2. Of those that a mesh axis runs over, the one named last changes fastest.
Arguments:
- inputs: bfloat16 [4, 1024, 1024], P('dp', ('blk', 'ulysses')), may hold values from -6 to 6
- gain_attn: float32 [1024], replicated, may hold values from 0.1 to 1.9
- query_key_value_weight: bfloat16 [1024, 2048], P(('dp', 'blk')), may hold values from -0.1875 to 0.1875
- w_out: bfloat16 [1024, 1024], P(('dp', 'blk')), may hold values from -4 to 4
- gain_mix: float32 [1024], replicated, may hold values from 0.1 to 1.9
- router: bfloat16 [1024, 16], replicated, may hold values from -0.09375 to 0.09375
- expert_in: bfloat16 [16, 1024, 1024], P(('dp', 'blk')), may hold values from -0.1875 to 0.1875
- expert_down: bfloat16 [16, 512, 1024], P(('dp', 'blk')), may hold values from -2 to 2
- routes: int32 [4, 1024, 8], P('dp', ('blk', 'ulysses')), may hold values from 0 to 15, all different within a row; in each aligned block of 128 rows (0 to 127, 128 to 255, ..., all dimensions but the last counted through in order) at most 80 rows name the same one
- cotangent: bfloat16 [4, 1024, 1024], P('dp', ('blk', 'ulysses')), may hold values from -6 to 6
Outputs:
- result: bfloat16 [4, 1024, 1024], P('dp', ('blk', 'ulysses'))
- input_grad: bfloat16 [4, 1024, 1024], P('dp', ('blk', 'ulysses'))
- grad_gain_attn: float32 [1024], replicated
- grad_w_qkv: float32 [1024, 2048], P(('dp', 'blk'))
- grad_w_out: float32 [1024, 1024], P(('dp', 'blk'))
- grad_gain_mix: float32 [1024], replicated
- grad_router: float32 [1024, 16], replicated
- grad_expert_in: float32 [16, 1024, 1024], P(('dp', 'blk'))
- grad_expert_down: float32 [16, 512, 1024], P(('dp', 'blk'))
The draws below stay inside these ranges and needn't reach their ends.
Inputs may be any that keep to these rules, and one draw needn't show every extreme that they name: `routes`: each row names 8 different experts. Within the 128 rows of one device no expert is named by more than 80 rows, and in some devices' rows one expert is named by exactly 80.
All inputs are finite; a program needn't handle non-finite values.
Results may differ from the reference program's by a relative error of at most 0.019.
Values may be sent and summed in bfloat16 or wider, within the bound.
A program may use at most 192 MiB of HBM per device.

```python
import math
import jax
import jax.numpy as jnp
import numpy as np
from jax import lax

MODEL_WIDTH = 1024
FF = 512
QUERY_HEADS = 16
KEY_VALUE_HEADS = 8
HEAD_SIZE = 64
EXPERTS = 16
TOP = 8
TOK_DEV = 128
SEQUENCE_LENGTH = 1024
SEQS = 4
CAPACITY = 80
KV_REP = 1
OUT_FAN = 2


def level_of(key, dims, cuts, low, largest):
    def one(dim, parts):
        heights = jax.random.uniform(jax.random.fold_in(jax.random.fold_in(key, 6), dim), (parts,), jnp.float32, low / len(cuts), largest / len(cuts))
        return jnp.repeat(jnp.exp(heights), dims[dim] // parts).reshape((-1,) + (1,) * (len(dims) - dim - 1))

    loudness = one(*cuts[0])
    for cut in cuts[1:]:
        loudness = loudness * one(*cut)
    return loudness


def assign_block(key, own, number, rows, amount, top, reach, skew):
    order = jax.random.permutation(key, amount)
    heavy_load, ordinary = load_shares(amount, rows * top, reach, skew, True), load_shares(amount, rows * top, reach, skew, False)
    places = jnp.arange(amount)

    def named(sizes, rotation):
        used = int((sizes > 0).sum())
        fixed = max(1, used // 4)
        passed = fixed + (places - fixed + rotation * (used - fixed)) % max(1, amount - fixed)
        return jnp.zeros((amount,), jnp.int32).at[order[jnp.where(places < fixed, places, passed)]].set(jnp.asarray(sizes, jnp.int32))

    sizes = jnp.where(number % 4 == 0, named(heavy_load, number // 4), named(ordinary, number - number // 4 - 1))
    mixed = jax.random.permutation(jax.random.fold_in(own, 3), amount)
    giver, sink = mixed[0:amount // 2 * 2:2], mixed[1:amount // 2 * 2:2]
    margin = jnp.minimum(sizes[giver] - 1, reach - sizes[sink]) // 2
    margin = jnp.where((giver == order[0]) | (sink == order[0]) | (sizes[sink] == 0), 0, jnp.maximum(margin, 0))
    passed = jax.random.randint(jax.random.fold_in(own, 4), (amount // 2,), 0, 1 << 20) % (margin + 1)
    sizes = sizes.at[giver].add(-passed).at[sink].add(passed)
    labels = jnp.searchsorted(jnp.cumsum(sizes), jnp.arange(rows * top), side="right").astype(jnp.int32)
    table = labels.reshape(top, rows).T
    table = table[jax.random.permutation(jax.random.fold_in(own, 1), rows)]
    rotation = jax.random.randint(jax.random.fold_in(own, 2), (rows, 1), 0, top)
    return jnp.take_along_axis(table, (jnp.arange(top)[None, :] + rotation) % top, axis=1)


def load_shares(count, total, reach, lean, full):
    loads = [(1 << 20) // math.isqrt(grade ** lean) + 1 for grade in range(1, count + 1)]
    largest = reach if full else min(reach, max(-(-total // count), total * loads[0] // sum(loads)))
    least = 1 if total - largest >= count - 1 else 0
    holding, spare = [largest] + [least] * (count - 1), total - largest - least * (count - 1)
    while spare > 0:
        free = [i for i in range(1, count) if holding[i] < largest] or [i for i in range(1, count) if holding[i] < reach]
        mass, budget = sum([loads[i] for i in free]), spare
        for i in free:
            extra = min(reach - holding[i], max(1, budget * loads[i] // mass), spare)
            holding[i] = holding[i] + extra
            spare = spare - extra
    return np.array(holding)


def scatter_about(stream_key, dims, spread, reach, cuts=(), kind=jnp.bfloat16):
    level = level_of(stream_key, dims, cuts, -0.22, 0.18) if cuts else 1.0
    entries = jax.random.normal(stream_key, dims, jnp.float32) * spread * level
    return jnp.minimum(jnp.maximum(entries, -reach), reach).astype(kind)


def setup_inputs(seed: int = 0) -> dict:
    key_of = jax.random.split(jax.random.key(seed), 11)
    inputs = scatter_about(key_of[0], (SEQS, SEQUENCE_LENGTH, MODEL_WIDTH), 1.0, 6.0, ((0, 4), (1, 8)))
    gain_attn = jnp.clip(1.0 + 0.18 * jax.random.normal(key_of[1], (MODEL_WIDTH,), jnp.float32), 0.1, 1.9)
    query_key_value_weight = scatter_about(key_of[2], (MODEL_WIDTH, QUERY_HEADS * HEAD_SIZE + 2 * KEY_VALUE_HEADS * HEAD_SIZE), MODEL_WIDTH ** -0.5, 0.1875, ((0, 8),))
    w_out = scatter_about(key_of[3], (MODEL_WIDTH, QUERY_HEADS * HEAD_SIZE), OUT_FAN ** -0.5, 4.0, ((0, 8),))
    gain_mix = jnp.clip(1.0 + 0.18 * jax.random.normal(key_of[4], (MODEL_WIDTH,), jnp.float32), 0.1, 1.9)
    router = scatter_about(key_of[5], (MODEL_WIDTH, EXPERTS), (4 * MODEL_WIDTH) ** -0.5, 0.09375)
    expert_in = scatter_about(key_of[6], (EXPERTS, MODEL_WIDTH, 2 * FF), MODEL_WIDTH ** -0.5, 0.1875, ((0, 8),))
    expert_down = scatter_about(key_of[7], (EXPERTS, FF, MODEL_WIDTH), (max(1, FF // 64)) ** -0.5, 2.0, ((0, 8),))
    routes_keys = jax.random.split(jax.random.fold_in(key_of[8], 1), SEQS * SEQUENCE_LENGTH // TOK_DEV)
    routes_turns = jax.random.permutation(jax.random.fold_in(key_of[8], 3), SEQS * SEQUENCE_LENGTH // TOK_DEV)
    routes = jax.vmap(lambda own, number: assign_block(jax.random.fold_in(key_of[8], 2), own, number, TOK_DEV, EXPERTS, TOP, CAPACITY, 1))(routes_keys, routes_turns).reshape((SEQS, SEQUENCE_LENGTH, TOP))
    cotangent = scatter_about(key_of[9], (SEQS, SEQUENCE_LENGTH, MODEL_WIDTH), 1.0, 6.0, ((0, 4), (1, 8)))
    return dict(inputs=inputs, gain_attn=gain_attn, query_key_value_weight=query_key_value_weight, w_out=w_out, gain_mix=gain_mix, router=router, expert_in=expert_in, expert_down=expert_down, routes=routes, cotangent=cotangent)


EPSILON = 1e-06
THETA = 10000.0
MASKED = -1e+30
HIGH = lax.Precision.HIGHEST

@jax.custom_vjp
def low(v):
    return lax.optimization_barrier(v.astype(jnp.bfloat16)).astype(jnp.float32)

@jax.custom_vjp
def low_back(v):
    return v

def low_keep(v):
    return (low(v), None)

def low_pass(kept, grad):
    return (grad,)

def back_keep(v):
    return (v, None)

def back_low(kept, grad):
    return (low(grad),)
low.defvjp(low_keep, low_pass)
low_back.defvjp(back_keep, back_low)

def rms_scale(values, gain):
    return values * lax.rsqrt(lax.optimization_barrier(jnp.mean(values * values, axis=-1, keepdims=True)) + EPSILON) * gain

def rotary_tables(positions, head_width):
    exponent = jnp.arange(head_width // 2, dtype=jnp.float32) * (2.0 / head_width)
    inverse = jnp.exp(-math.log(THETA) * exponent)
    angles = positions.astype(jnp.float32)[:, None] * inverse[None, :]
    return (jnp.cos(angles)[:, None, :], jnp.sin(angles)[:, None, :])

def rotate(values, cosine, sine):
    half_size = values.shape[-1] // 2
    first_half = values[..., :half_size]
    second_half = values[..., half_size:]
    return jnp.concatenate([first_half * cosine - second_half * sine, second_half * cosine + first_half * sine], axis=-1)

def attend(queries, all_keys, all_values):
    length = queries.shape[0]
    repeated_heads = all_keys.shape[1]
    grouped = queries.reshape(length, repeated_heads, queries.shape[1] // repeated_heads, HEAD_SIZE)
    row_block = min(512, length)
    score_scale = HEAD_SIZE ** (-0.5)
    key_pos = jnp.arange(length, dtype=jnp.int32)

    def one_block(offset):
        row_part = lax.dynamic_slice_in_dim(grouped, offset, row_block, 0)
        scores = low_back(jnp.einsum('qrgd,krd->qrgk', row_part, all_keys, precision=HIGH) * score_scale)
        query_here = offset + jnp.arange(row_block, dtype=jnp.int32)
        allowed = key_pos[None, :] <= query_here[:, None]
        scores = jnp.where(allowed[:, None, None, :], scores, MASKED)
        weights_all = jax.nn.softmax(scores, axis=-1)
        return jnp.einsum('qrgk,krd->qrgd', low(weights_all), all_values, precision=HIGH)
    offsets = jnp.arange(length // row_block, dtype=jnp.int32) * row_block
    mixed_blocks = lax.map(jax.checkpoint(one_block), offsets)
    return mixed_blocks.reshape(length, -1)

def route_slots(block_routes):
    flat_routes = block_routes.reshape(-1)
    marks = (flat_routes[:, None] == jnp.arange(EXPERTS, dtype=jnp.int32)[None, :]).astype(jnp.int32)
    filled = jnp.cumsum(marks, axis=0)
    slot_number = lax.optimization_barrier(jnp.sum(marks * filled, axis=1)) - 1
    slot_index = flat_routes * CAPACITY + slot_number
    token_ids = jnp.arange(flat_routes.shape[0], dtype=jnp.int32) // TOP
    slot_owner = jnp.full((EXPERTS * CAPACITY,), TOK_DEV, jnp.int32).at[slot_index].set(token_ids)
    return (slot_index, slot_owner)

def take_rows(table, row_ids):
    return table[row_ids]

def layer(layer_in, weights, seq_routes):
    gain_attn, query_key_value_weight, w_out, gain_mix, router, expert_in, expert_down = weights
    query_columns = QUERY_HEADS * HEAD_SIZE
    key_value_columns = KEY_VALUE_HEADS * HEAD_SIZE
    norm_attn = low(rms_scale(layer_in, gain_attn))
    projected_rows = low_back(jnp.dot(norm_attn, query_key_value_weight, precision=HIGH))
    cosine, sine = rotary_tables(jnp.arange(SEQUENCE_LENGTH, dtype=jnp.int32), HEAD_SIZE)
    q_raw = projected_rows[:, :query_columns].reshape(SEQUENCE_LENGTH, QUERY_HEADS, HEAD_SIZE)
    key_plain = projected_rows[:, query_columns:query_columns + key_value_columns].reshape(SEQUENCE_LENGTH, KEY_VALUE_HEADS, HEAD_SIZE)
    value_plain = projected_rows[:, query_columns + key_value_columns:].reshape(SEQUENCE_LENGTH, KEY_VALUE_HEADS, HEAD_SIZE)
    queries = low(low_back(rotate(q_raw, cosine, sine)))
    all_keys = low(low_back(jnp.repeat(rotate(key_plain, cosine, sine), KV_REP, axis=1)))
    all_values = low(low_back(jnp.repeat(value_plain, KV_REP, axis=1)))
    attn_mixed = low(low_back(attend(queries, all_keys, all_values)))
    branch = low_back(jnp.dot(attn_mixed, w_out.T, precision=HIGH))
    residual = layer_in + branch
    norm_mix = low(rms_scale(residual, gain_mix))
    logits = jnp.dot(norm_mix, router, precision=HIGH)
    route_picks = (seq_routes[:, :, None] == jnp.arange(EXPERTS, dtype=jnp.int32)[None, None, :]).astype(jnp.float32)
    chosen = lax.optimization_barrier(jnp.sum(route_picks * logits[:, None, :], axis=-1))
    gate_values = jax.nn.softmax(chosen, axis=-1)
    blocks = SEQUENCE_LENGTH // TOK_DEV
    slot_index, slot_owner = jax.vmap(route_slots)(seq_routes.reshape(blocks, TOK_DEV, TOP))
    padded = jnp.concatenate([norm_mix.reshape(blocks, TOK_DEV, MODEL_WIDTH), jnp.zeros((blocks, 1, MODEL_WIDTH), jnp.float32)], axis=1)
    dispatched = jax.vmap(take_rows)(padded, slot_owner).reshape(blocks, EXPERTS, CAPACITY, MODEL_WIDTH)
    both_halves = low_back(jnp.einsum('becd,edf->becf', dispatched, expert_in, precision=HIGH))
    hidden = low(jax.nn.silu(both_halves[..., :FF]) * both_halves[..., FF:])
    expert_out = low_back(jnp.einsum('bech,ehd->becd', hidden, expert_down, precision=HIGH))
    routed = jax.vmap(take_rows)(expert_out.reshape(blocks, EXPERTS * CAPACITY, MODEL_WIDTH), slot_index).reshape(SEQUENCE_LENGTH, TOP, MODEL_WIDTH)
    return residual + lax.optimization_barrier(jnp.sum(gate_values[..., None] * routed, axis=1))

def reference(inputs, gain_attn, query_key_value_weight, w_out, gain_mix, router, expert_in, expert_down, routes, cotangent):
    params = tuple((weight.astype(jnp.float32) for weight in (gain_attn, query_key_value_weight, w_out, gain_mix, router, expert_in, expert_down)))

    def one_sequence(totals, seq_item):
        seq_in, seq_routes, seq_cot = seq_item

        def forward(layer_in, *weights):
            return layer(layer_in, weights, seq_routes)
        layer_out, pullback = jax.vjp(forward, seq_in.astype(jnp.float32), *params)
        grad_list = pullback(seq_cot.astype(jnp.float32))
        totals = tuple((running + grad_part for running, grad_part in zip(totals, grad_list[1:])))
        return (totals, (layer_out.astype(jnp.bfloat16), grad_list[0].astype(jnp.bfloat16)))
    zeros_init = tuple((jnp.zeros_like(weight) for weight in params))
    totals, (outputs, input_grads) = lax.scan(one_sequence, zeros_init, (inputs, routes, cotangent))
    return (outputs, input_grads, totals[0], totals[1], totals[2], totals[3], totals[4], totals[5], totals[6])
```

```python
import functools
import math

import jax
import jax.numpy as jnp
from jax import lax
from jax.experimental import pallas as pl
from jax.experimental.pallas import tpu as pltpu
from jax.sharding import PartitionSpec as P

QUERY_HEADS = 16
KEY_VALUE_HEADS = 8
HEAD_SIZE = 64
CAPACITY = 80


EPSILON = 1e-06
THETA = 10000.0
MASKED = -1e30


def passed_along(value, axis, steps):
    count = lax.axis_size(axis)
    initial, last = (max(0, -steps), min(count, count - steps))
    return lax.ppermute(value, axis, [(source, source + steps) for source in range(initial, last)])


def rms_scale(values, gain):
    return values * lax.rsqrt(jnp.mean(values * values, axis=-1, keepdims=True) + EPSILON) * gain


def rotary_tables(positions, head_width):
    exponent = jnp.arange(head_width // 2, dtype=jnp.float32) * (2.0 / head_width)
    inverse = jnp.exp(-math.log(THETA) * exponent)
    angles = positions.astype(jnp.float32)[:, None] * inverse[None, :]
    return (jnp.cos(angles)[:, None, :], jnp.sin(angles)[:, None, :])


def rotate(values, cosine, sine):
    half_size = values.shape[-1] // 2
    first_half = values[..., :half_size]
    second_half = values[..., half_size:]
    return jnp.concatenate(
        [first_half * cosine - second_half * sine, second_half * cosine + first_half * sine],
        axis=-1,
    )


def rotate_back(grad_values, cosine, sine):
    half_size = grad_values.shape[-1] // 2
    first_half = grad_values[..., :half_size]
    second_half = grad_values[..., half_size:]
    return jnp.concatenate(
        [first_half * cosine + second_half * sine, second_half * cosine - first_half * sine],
        axis=-1,
    )


def attend_forward(queries, all_keys, all_values, query_pos, key_pos, key_ok, row_block):
    score_scale = queries.shape[-1] ** (-0.5)
    block_count = queries.shape[0] // row_block

    def one_block(block_index):
        offset = block_index * row_block
        row_part = lax.dynamic_slice_in_dim(queries, offset, row_block, 0)
        query_here = lax.dynamic_slice_in_dim(query_pos, offset, row_block, 0)
        scores = (
            jnp.einsum("qrgd,krd->qrgk", row_part, all_keys, preferred_element_type=jnp.float32)
            * score_scale
        )
        allowed = (key_pos[None, :] <= query_here[:, None]) & key_ok[None, :]
        scores = jnp.where(allowed[:, None, None, :], scores, MASKED)
        row_peak = jnp.max(scores, axis=-1, keepdims=True)
        exps_all = jnp.exp(scores - row_peak)
        row_total = jnp.sum(exps_all, axis=-1, keepdims=True)
        weights_low = (exps_all / row_total).astype(jnp.bfloat16)
        mixed_part = jnp.einsum(
            "qrgk,krd->qrgd", weights_low, all_values, preferred_element_type=jnp.float32
        )
        return (mixed_part, (row_peak + jnp.log(row_total))[..., 0])

    mixed_blocks, log_sums = lax.map(one_block, jnp.arange(block_count, dtype=jnp.int32))
    return (mixed_blocks.reshape(queries.shape), log_sums.reshape(queries.shape[:3]))


def attend_backward(
    queries, all_keys, all_values, query_pos, key_pos, key_ok, log_sums, mixed_grad, row_block
):
    score_scale = queries.shape[-1] ** (-0.5)
    block_count = queries.shape[0] // row_block

    def one_block(carry, block_index):
        key_grads, value_grads = carry
        offset = block_index * row_block
        row_part = lax.dynamic_slice_in_dim(queries, offset, row_block, 0)
        query_here = lax.dynamic_slice_in_dim(query_pos, offset, row_block, 0)
        grad_part = lax.dynamic_slice_in_dim(mixed_grad, offset, row_block, 0)
        sums_part = lax.dynamic_slice_in_dim(log_sums, offset, row_block, 0)
        scores = (
            jnp.einsum("qrgd,krd->qrgk", row_part, all_keys, preferred_element_type=jnp.float32)
            * score_scale
        )
        allowed = (key_pos[None, :] <= query_here[:, None]) & key_ok[None, :]
        scores = jnp.where(allowed[:, None, None, :], scores, MASKED)
        probs_all = jnp.exp(scores - sums_part[..., None])
        value_grads = value_grads + jnp.einsum(
            "qrgk,qrgd->krd",
            probs_all.astype(jnp.bfloat16),
            grad_part,
            preferred_element_type=jnp.float32,
        )
        probs_grad = jnp.einsum(
            "qrgd,krd->qrgk", grad_part, all_values, preferred_element_type=jnp.float32
        )
        score_grad = probs_all * (
            probs_grad - jnp.sum(probs_all * probs_grad, axis=-1, keepdims=True)
        )
        score_low = score_grad.astype(jnp.bfloat16)
        row_grads = (
            jnp.einsum("qrgk,krd->qrgd", score_low, all_keys, preferred_element_type=jnp.float32)
            * score_scale
        )
        key_grads = (
            key_grads
            + jnp.einsum("qrgk,qrgd->krd", score_low, row_part, preferred_element_type=jnp.float32)
            * score_scale
        )
        return ((key_grads, value_grads), row_grads)

    zero_grads = jnp.zeros(all_keys.shape, jnp.float32)
    (key_grads, value_grads), row_grads = lax.scan(
        one_block, (zero_grads, zero_grads), jnp.arange(block_count, dtype=jnp.int32)
    )
    return (row_grads.reshape(queries.shape), key_grads, value_grads)


MESH = pl.DeviceIdType.MESH
TOKEN_AXES = ("ulysses",)
EXPERT_AXES = ("dp", "blk")
VMEM_LIMIT = 40 * 1024 * 1024


def flat_index(axes, sizes):
    index = lax.axis_index(axes[0])
    for axis, size in zip(axes[1:], sizes[1:]):
        index = index * size + lax.axis_index(axis)
    return index


def device_of(axes, sizes, index):
    place = {}
    for axis, size in zip(reversed(axes), reversed(sizes)):
        place[axis] = lax.rem(index, size)
        index = index // size
    return place


def greet(places):
    barrier = pltpu.get_barrier_semaphore()
    for place in places:
        pl.semaphore_signal(barrier, inc=1, device_id=place, device_id_type=MESH)
    pl.semaphore_wait(barrier, len(places))


def remote(source, target, send, recv, place):
    return pltpu.make_async_remote_copy(
        src_ref=source,
        dst_ref=target,
        send_sem=send,
        recv_sem=recv,
        device_id=place,
        device_id_type=MESH,
    )


def direct_copies(axes, sizes, personal, ins, outs, send, recv, local):
    count = math.prod(sizes)
    me = flat_index(axes, sizes)
    copies = []
    for step in range(1, count):
        other = lax.rem(me + step, count)
        place = device_of(axes, sizes, other)
        for item, (source, target) in enumerate(zip(ins, outs)):
            copies.append(
                remote(
                    source.at[other] if personal[item] else source,
                    target.at[me],
                    send.at[item, step],
                    recv.at[item, step],
                    place,
                )
            )
    for item, (source, target) in enumerate(zip(ins, outs)):
        copies.append(
            pltpu.make_async_copy(
                source.at[me] if personal[item] else source, target.at[me], local.at[item]
            )
        )
    return copies


def other_places(axes, sizes):
    count = math.prod(sizes)
    me = flat_index(axes, sizes)
    return [device_of(axes, sizes, lax.rem(me + step, count)) for step in range(1, count)]


def exchange_kernel(axes, sizes, personal, *refs):
    count = len(personal)
    ins, outs = refs[:count], refs[count : 2 * count]
    send, recv, local = refs[2 * count :]
    greet(other_places(axes, sizes))
    copies = direct_copies(axes, sizes, personal, ins, outs, send, recv, local)
    for copy in copies:
        copy.start()
    for copy in copies:
        copy.wait()


def exchange(values, personal, axes, sizes, collective_id):
    count = math.prod(sizes)
    shapes = [
        jax.ShapeDtypeStruct(value.shape if one else (count,) + value.shape, value.dtype)
        for value, one in zip(values, personal)
    ]
    total = len(values)
    return pl.pallas_call(
        functools.partial(exchange_kernel, axes, sizes, personal),
        out_shape=shapes,
        in_specs=[pl.BlockSpec(memory_space=pl.ANY)] * total,
        out_specs=[pl.BlockSpec(memory_space=pl.ANY)] * total,
        scratch_shapes=[
            pltpu.SemaphoreType.DMA((total, count)),
            pltpu.SemaphoreType.DMA((total, count)),
            pltpu.SemaphoreType.DMA((total,)),
        ],
        compiler_params=pltpu.CompilerParams(collective_id=collective_id, has_side_effects=True),
    )(*values)


def gather_kernel(sizes, token_sizes, wide, near, *refs):
    total = wide + near
    ins, outs = refs[:total], refs[total : 2 * total]
    line_send, line_recv, side_send, side_recv, local, near_send, near_recv, near_local = refs[
        2 * total :
    ]
    line, pair = sizes
    here, side = lax.axis_index("dp"), lax.axis_index("blk")
    me = here * pair + side
    across = {"blk": 1 - side}
    places = [{"dp": lax.rem(here + step, line)} for step in range(1, line)]
    greet(places + [across] + (other_places(TOKEN_AXES, token_sizes) if near else []))
    waits = []
    for item in range(wide):
        for step in range(line - 1, 0, -1):
            copy = remote(
                ins[item],
                outs[item].at[me],
                line_send.at[item, step],
                line_recv.at[item, step],
                places[step - 1],
            )
            copy.start()
        copy = remote(
            ins[item], outs[item].at[me], side_send.at[item, 0], side_recv.at[item, 0], across
        )
        copy.start()
        waits.append(copy)
        copy = pltpu.make_async_copy(ins[item], outs[item].at[me], local.at[item])
        copy.start()
        waits.append(copy)
    if near:
        for copy in direct_copies(
            TOKEN_AXES,
            token_sizes,
            (False,) * near,
            ins[wide:],
            outs[wide:],
            near_send,
            near_recv,
            near_local,
        ):
            copy.start()
            waits.append(copy)
    for step in range(1, line):
        for item in range(wide):
            arrived = remote(
                ins[item],
                outs[item].at[me],
                line_send.at[item, step],
                line_recv.at[item, step],
                places[step - 1],
            )
            arrived.wait()
            block = lax.rem(here + line - step, line) * pair + side
            copy = remote(
                outs[item].at[block],
                outs[item].at[block],
                side_send.at[item, step],
                side_recv.at[item, step],
                across,
            )
            copy.start()
            waits.append(copy)
    for copy in waits:
        copy.wait()


def gather_wide(values, near_values, sizes, token_sizes, collective_id):
    count = math.prod(sizes)
    near_count = math.prod(token_sizes)
    wide, near = len(values), len(near_values)
    shapes = [jax.ShapeDtypeStruct((count,) + value.shape, value.dtype) for value in values]
    shapes += [
        jax.ShapeDtypeStruct((near_count,) + value.shape, value.dtype) for value in near_values
    ]
    return pl.pallas_call(
        functools.partial(gather_kernel, sizes, token_sizes, wide, near),
        out_shape=shapes,
        in_specs=[pl.BlockSpec(memory_space=pl.ANY)] * (wide + near),
        out_specs=[pl.BlockSpec(memory_space=pl.ANY)] * (wide + near),
        scratch_shapes=[
            pltpu.SemaphoreType.DMA((wide, sizes[0])),
            pltpu.SemaphoreType.DMA((wide, sizes[0])),
            pltpu.SemaphoreType.DMA((wide, sizes[0])),
            pltpu.SemaphoreType.DMA((wide, sizes[0])),
            pltpu.SemaphoreType.DMA((wide,)),
            pltpu.SemaphoreType.DMA((max(near, 1), near_count)),
            pltpu.SemaphoreType.DMA((max(near, 1), near_count)),
            pltpu.SemaphoreType.DMA((max(near, 1),)),
        ],
        compiler_params=pltpu.CompilerParams(collective_id=collective_id, has_side_effects=True),
    )(*values, *near_values)


def reduce_kernel(sizes, total, personal, *refs):
    small = len(personal)
    ins, refs = refs[:total], refs[total:]
    small_ins, refs = refs[:small], refs[small:]
    outs, refs = refs[:total], refs[total:]
    small_outs, refs = refs[:small], refs[small:]
    side_bufs, refs = refs[:total], refs[total:]
    sent_bufs, refs = refs[:total], refs[total:]
    line_bufs, refs = refs[:total], refs[total:]
    side_send, side_recv, line_send, line_recv, send, recv, local = refs
    line, pair = sizes
    here, side = lax.axis_index("dp"), lax.axis_index("blk")
    across = {"blk": 1 - side}
    greet(other_places(EXPERT_AXES, sizes))

    def side_copy(item, step):
        target = lax.rem(here + step, line)
        return remote(
            ins[item].at[target * pair + 1 - side],
            side_bufs[item].at[step],
            side_send.at[item, step],
            side_recv.at[item, step],
            across,
        )

    def line_copy(item, step):
        return remote(
            sent_bufs[item].at[step],
            line_bufs[item].at[step],
            line_send.at[item, step],
            line_recv.at[item, step],
            {"dp": lax.rem(here + step, line)},
        )

    order = list(range(1, line)) + [0]
    for step in order:
        for item in range(total):
            side_copy(item, step).start()
    copies = direct_copies(
        EXPERT_AXES, sizes, personal, small_ins, small_outs, send, recv, local
    )
    for copy in copies:
        copy.start()
    for step in order:
        for item in range(total):
            side_copy(item, step).wait()
            block = lax.rem(here + step, line) * pair + side
            both = ins[item][block].astype(jnp.float32) + side_bufs[item][step].astype(jnp.float32)
            if step:
                sent_bufs[item][step] = both.astype(jnp.bfloat16)
                line_copy(item, step).start()
            else:
                outs[item][...] = both
    for step in range(1, line):
        for item in range(total):
            line_copy(item, step).wait()
            outs[item][...] += line_bufs[item][step].astype(jnp.float32)
    for copy in copies:
        copy.wait()


def reduce_wide(values, small_values, personal, sizes, collective_id):
    count = math.prod(sizes)
    total, small = len(values), len(small_values)
    shapes = [jax.ShapeDtypeStruct(value.shape[1:], jnp.float32) for value in values]
    shapes += [
        jax.ShapeDtypeStruct(value.shape if one else (count,) + value.shape, value.dtype)
        for value, one in zip(small_values, personal)
    ]
    buffers = [pltpu.VMEM((sizes[0],) + value.shape[1:], jnp.bfloat16) for value in values]
    wide_sems = pltpu.SemaphoreType.DMA((total, sizes[0]))
    return pl.pallas_call(
        functools.partial(reduce_kernel, sizes, total, personal),
        out_shape=shapes,
        in_specs=[pl.BlockSpec(memory_space=pltpu.VMEM)] * (total + small),
        out_specs=[pl.BlockSpec(memory_space=pltpu.VMEM)] * (total + small),
        scratch_shapes=buffers * 3
        + [wide_sems] * 4
        + [
            pltpu.SemaphoreType.DMA((small, count)),
            pltpu.SemaphoreType.DMA((small, count)),
            pltpu.SemaphoreType.DMA((small,)),
        ],
        compiler_params=pltpu.CompilerParams(
            collective_id=collective_id, has_side_effects=True, vmem_limit_bytes=VMEM_LIMIT
        ),
    )(*values, *small_values)


def dense_gates(logits, mask):
    masked = jnp.where(mask, logits, MASKED)
    exps = jnp.where(mask, jnp.exp(masked - jnp.max(masked, axis=-1, keepdims=True)), 0.0)
    return exps / jnp.sum(exps, axis=-1, keepdims=True)


def body(
    inputs,
    gain_attn,
    query_key_value_weight,
    w_out,
    gain_mix,
    router,
    expert_in,
    expert_down,
    routes,
    cotangent,
):
    cycle_size = lax.axis_size("blk")
    slice_total = lax.axis_size("ulysses")
    sizes = (lax.axis_size("dp"), cycle_size)
    token_sizes = (slice_total,)
    groups = math.prod(sizes)
    cycle_index = lax.axis_index("blk")
    slice_index = lax.axis_index("ulysses")
    token_rows = inputs.shape[1]
    width = inputs.shape[2]
    head_width = HEAD_SIZE
    head_copies = max(1, slice_total // KEY_VALUE_HEADS)
    repeated_heads = KEY_VALUE_HEADS * head_copies
    group_size = QUERY_HEADS // repeated_heads
    local_rep = repeated_heads // slice_total
    local_query = QUERY_HEADS // slice_total
    span_len = token_rows * slice_total
    row_block = min(512, span_len)
    query_columns = QUERY_HEADS * head_width
    key_value_columns = KEY_VALUE_HEADS * head_width
    query_part = local_query * head_width
    pair_part = local_rep * head_width
    num_experts = router.shape[1]
    held = expert_in.shape[0]
    hidden_units = expert_down.shape[1]
    bf16 = jnp.bfloat16
    f32 = jnp.float32

    layer_in = inputs[0].astype(f32)
    norm_attn = rms_scale(layer_in, gain_attn).astype(bf16)
    mask = jnp.any(
        routes[0][:, :, None] == jnp.arange(num_experts, dtype=jnp.int32)[None, None, :], axis=1
    )
    query_start = slice_index * query_part
    pair_start = (slice_index * local_rep) // head_copies * head_width
    weight_part = jnp.concatenate(
        [
            lax.dynamic_slice_in_dim(query_key_value_weight, query_start, query_part, 1),
            lax.dynamic_slice_in_dim(
                query_key_value_weight, query_columns + pair_start, pair_part, 1
            ),
            lax.dynamic_slice_in_dim(
                query_key_value_weight,
                query_columns + key_value_columns + pair_start,
                pair_part,
                1,
            ),
            lax.dynamic_slice_in_dim(w_out, query_start, query_part, 1),
        ],
        axis=1,
    )
    weight_blocks, mask_blocks, norm_blocks = gather_wide(
        [weight_part, mask.astype(bf16).T], [norm_attn], sizes, token_sizes, 0
    )
    held_cotangent = lax.all_gather(cotangent[0], EXPERT_AXES, axis=0, tiled=True)
    weights = weight_blocks.reshape(width, -1)
    own_columns = query_part + 2 * pair_part
    qkv_weight = weights[:, :own_columns]
    out_weight = weights[:, own_columns:]
    span_norm = norm_blocks.reshape(span_len, width)
    projected = jnp.dot(span_norm, qkv_weight, preferred_element_type=f32)
    span_rows = jnp.arange(span_len, dtype=jnp.int32)
    query_pos = cycle_index * span_len + span_rows
    cosine, sine = rotary_tables(query_pos, head_width)
    q_raw = projected[:, :query_part].reshape(span_len, local_query, head_width)
    key_plain = projected[:, query_part : query_part + pair_part].reshape(
        span_len, local_rep, head_width
    )
    value_plain = projected[:, query_part + pair_part :].reshape(span_len, local_rep, head_width)
    queries = (
        rotate(q_raw, cosine, sine)
        .astype(bf16)
        .reshape(span_len, local_rep, group_size, head_width)
    )
    own_pair = jnp.stack([rotate(key_plain, cosine, sine).astype(bf16), value_plain.astype(bf16)])
    earlier_pair = passed_along(own_pair, "blk", 1)
    all_keys = jnp.concatenate([own_pair[0], earlier_pair[0]], axis=0)
    all_values = jnp.concatenate([own_pair[1], earlier_pair[1]], axis=0)
    key_pos = jnp.concatenate(
        [(cycle_index - cycle_step) * span_len + span_rows for cycle_step in range(cycle_size)]
    )
    key_ok = jnp.concatenate(
        [
            jnp.broadcast_to(cycle_index - cycle_step >= 0, (span_len,))
            for cycle_step in range(cycle_size)
        ]
    )
    attn_heads, log_sums = attend_forward(
        queries, all_keys, all_values, query_pos, key_pos, key_ok, row_block
    )
    mixed = attn_heads.astype(bf16).reshape(span_len, query_part)
    branch_part = lax.dot_general(
        mixed, out_weight, (((1,), (1,)), ((), ())), preferred_element_type=f32
    )
    (branch_blocks,) = exchange(
        [branch_part.astype(bf16).reshape(slice_total, token_rows, width)],
        (True,),
        TOKEN_AXES,
        token_sizes,
        1,
    )
    residual = layer_in + jnp.sum(branch_blocks.astype(f32), axis=0)
    norm_mix = rms_scale(residual, gain_mix).astype(bf16)
    (mix_blocks,) = gather_wide([norm_mix], [], sizes, token_sizes, 2)

    rows = mix_blocks.reshape(groups * token_rows, width)
    row_mask = jnp.swapaxes(mask_blocks, 1, 2).reshape(groups * token_rows, num_experts) > 0
    row_gates = dense_gates(jnp.dot(rows, router, preferred_element_type=f32), row_mask)
    first_held = flat_index(EXPERT_AXES, sizes) * held
    own_gates = lax.dynamic_slice_in_dim(row_gates, first_held, held, 1)
    row_grad = held_cotangent.astype(f32)
    combined = 0.0
    gate_grads, both_list, in_terms, down_terms = [], [], [], []
    for expert in range(held):
        weight_in, weight_down = expert_in[expert], expert_down[expert]
        gate = own_gates[:, expert : expert + 1]
        both_halves = jnp.dot(rows, weight_in, preferred_element_type=f32)
        gate_half = both_halves[:, :hidden_units]
        up_half = both_halves[:, hidden_units:]
        sigmoid_gate = jax.nn.sigmoid(gate_half)
        activated = gate_half * sigmoid_gate
        hidden = (activated * up_half).astype(bf16)
        expert_out = jnp.dot(hidden, weight_down, preferred_element_type=f32)
        combined = combined + gate * expert_out
        gate_grads.append(jnp.sum(row_grad * expert_out, axis=-1))
        expert_grad = (gate * row_grad).astype(bf16)
        hidden_grad = lax.dot_general(
            expert_grad, weight_down, (((1,), (1,)), ((), ())), preferred_element_type=f32
        )
        gate_half_grad = (
            hidden_grad * up_half * sigmoid_gate * (1.0 + gate_half * (1.0 - sigmoid_gate))
        )
        both_grad = jnp.concatenate([gate_half_grad, hidden_grad * activated], axis=-1).astype(
            bf16
        )
        both_list.append(both_grad)
        in_terms.append((rows, both_grad))
        down_terms.append((hidden, expert_grad))
    dispatch_sum = sum(
        lax.dot_general(
            both_list[expert],
            expert_in[expert],
            (((1,), (1,)), ((), ())),
            preferred_element_type=f32,
        )
        for expert in range(held)
    )

    def weight_term(pairs):
        return jnp.concatenate(
            [
                lax.dot_general(
                    left, right, (((0,), (0,)), ((), ())), preferred_element_type=f32
                ).astype(bf16)
                for left, right in pairs
            ],
            axis=0,
        )

    gate_rows = jnp.stack(gate_grads + [jnp.zeros_like(gate_grads[0])] * (-held % 8))
    gate_send = jnp.swapaxes(gate_rows.reshape(-1, groups, token_rows), 0, 1)
    combined_sum, mix_grad, gate_blocks = reduce_wide(
        [
            combined.astype(bf16).reshape(groups, token_rows, width),
            dispatch_sum.astype(bf16).reshape(groups, token_rows, width),
        ],
        [gate_send],
        (True,),
        sizes,
        3,
    )
    in_part = lax.psum_scatter(
        weight_term(in_terms), "ulysses", scatter_dimension=0, tiled=True
    )
    down_part = lax.psum_scatter(
        weight_term(down_terms), "ulysses", scatter_dimension=0, tiled=True
    )
    grad_expert_in = (
        lax.all_gather(in_part, "ulysses", axis=0, tiled=True)
        .astype(f32)
        .reshape(expert_in.shape)
    )
    grad_expert_down = (
        lax.all_gather(down_part, "ulysses", axis=0, tiled=True)
        .astype(f32)
        .reshape(expert_down.shape)
    )

    result = (residual + combined_sum).astype(bf16)
    out_grad = cotangent[0].astype(f32)
    gate_values = dense_gates(jnp.dot(norm_mix, router, preferred_element_type=f32), mask)
    gate_grad = gate_blocks[:, :held, :].reshape(num_experts, token_rows).T
    logit_grad = gate_values * (
        gate_grad - jnp.sum(gate_values * gate_grad, axis=-1, keepdims=True)
    )
    mix_grad = mix_grad + jnp.dot(
        logit_grad, router.astype(f32).T, precision=lax.Precision.HIGHEST
    )
    router_grad = jnp.dot(
        logit_grad.T, norm_mix.astype(f32), precision=lax.Precision.HIGHEST
    )
    _, mix_back = jax.vjp(rms_scale, residual, gain_mix)
    residual_norm_grad, gain_mix_grad = mix_back(mix_grad)
    residual_grad = out_grad + residual_norm_grad
    branch_grad = residual_grad.astype(bf16)
    shared = jnp.concatenate([router_grad, gain_mix_grad[None]], axis=0)
    shared = jnp.pad(shared, ((0, -shared.shape[0] % 8), (0, 0)))
    shared_rows = shared.shape[0]
    shared_send = jnp.swapaxes(shared.reshape(shared_rows, slice_total, -1), 0, 1)
    grad_blocks, shared_blocks = exchange(
        [branch_grad, shared_send], (False, True), TOKEN_AXES, token_sizes, 4
    )
    span_grad = grad_blocks.reshape(span_len, width)
    shared_part = jnp.sum(shared_blocks, axis=0)
    mixed_grad = (
        jnp.dot(span_grad, out_weight, preferred_element_type=f32)
        .astype(bf16)
        .reshape(span_len, local_rep, group_size, head_width)
    )
    query_grad, key_grads, value_grads = attend_backward(
        queries, all_keys, all_values, query_pos, key_pos, key_ok, log_sums, mixed_grad, row_block
    )
    pair_grads = jnp.stack([key_grads, value_grads]).reshape(
        2, cycle_size, span_len, local_rep, head_width
    )
    own_grads = pair_grads[:, 0] + passed_along(
        pair_grads[:, 1].astype(bf16), "blk", -1
    ).astype(f32)
    own_grads = own_grads.astype(bf16).astype(f32)
    dq_raw = rotate_back(
        query_grad.astype(bf16).astype(f32).reshape(span_len, local_query, head_width),
        cosine,
        sine,
    )
    dk_raw = rotate_back(own_grads[0], cosine, sine)
    qkv_grad = jnp.concatenate(
        [
            dq_raw.reshape(span_len, query_part),
            dk_raw.reshape(span_len, pair_part),
            own_grads[1].reshape(span_len, pair_part),
        ],
        axis=1,
    ).astype(bf16)
    norm_grad_part = lax.dot_general(
        qkv_grad, qkv_weight, (((1,), (1,)), ((), ())), preferred_element_type=f32
    )
    (norm_grad_blocks,) = exchange(
        [norm_grad_part.astype(bf16).reshape(slice_total, token_rows, width)],
        (True,),
        TOKEN_AXES,
        token_sizes,
        5,
    )
    attn_norm_grad = jnp.sum(norm_grad_blocks.astype(f32), axis=0)
    _, attn_back = jax.vjp(rms_scale, layer_in, gain_attn)
    input_norm_grad, gain_attn_grad = attn_back(attn_norm_grad)
    input_grad = (residual_grad + input_norm_grad).astype(bf16)
    weight_grads = jnp.concatenate(
        [
            lax.dot_general(
                span_norm, qkv_grad, (((0,), (0,)), ((), ())), preferred_element_type=f32
            ),
            lax.dot_general(
                span_grad, mixed, (((0,), (0,)), ((), ())), preferred_element_type=f32
            ),
        ],
        axis=1,
    ).astype(bf16)
    weight_sum, shared_blocks, gain_blocks = reduce_wide(
        [weight_grads.reshape(groups, width // groups, -1)],
        [shared_part, gain_attn_grad.reshape(8, -1)],
        (False, False),
        sizes,
        6,
    )
    weight_blocks, shared_blocks, gain_blocks = exchange(
        [
            weight_sum.astype(bf16),
            jnp.sum(shared_blocks, axis=0),
            jnp.sum(gain_blocks, axis=0),
        ],
        (False, False, False),
        TOKEN_AXES,
        token_sizes,
        7,
    )
    weight_blocks = weight_blocks.astype(f32)

    def columns(first, count, copies):
        part = weight_blocks[:, :, first : first + count]
        part = part.reshape(slice_total // copies, copies, part.shape[1], count)
        return jnp.swapaxes(jnp.sum(part, axis=1), 0, 1).reshape(part.shape[2], -1)

    grad_w_qkv = jnp.concatenate(
        [
            columns(0, query_part, 1),
            columns(query_part, pair_part, head_copies),
            columns(query_part + pair_part, pair_part, head_copies),
        ],
        axis=1,
    )
    grad_w_out = columns(own_columns, query_part, 1)
    shared_sum = jnp.swapaxes(shared_blocks, 0, 1).reshape(shared_rows, width)
    return (
        result[None],
        input_grad[None],
        jnp.sum(gain_blocks, axis=0).reshape(width),
        grad_w_qkv,
        grad_w_out,
        shared_sum[num_experts],
        shared_sum[:num_experts].T,
        grad_expert_in,
        grad_expert_down,
    )


def solution(mesh):
    in_specs = (
        P("dp", ("blk", "ulysses"), None),
        P(),
        P(("dp", "blk"), None),
        P(("dp", "blk"), None),
        P(),
        P(),
        P(("dp", "blk"), None, None),
        P(("dp", "blk"), None, None),
        P("dp", ("blk", "ulysses"), None),
        P("dp", ("blk", "ulysses"), None),
    )
    out_specs = (
        P("dp", ("blk", "ulysses"), None),
        P("dp", ("blk", "ulysses"), None),
        P(),
        P(("dp", "blk"), None),
        P(("dp", "blk"), None),
        P(),
        P(),
        P(("dp", "blk"), None, None),
        P(("dp", "blk"), None, None),
    )
    return jax.shard_map(body, mesh=mesh, in_specs=in_specs, out_specs=out_specs, check_vma=False)
```

```python
import functools
import math

import jax
import jax.numpy as jnp
from jax import lax
from jax.experimental import pallas as pl
from jax.experimental.pallas import tpu as pltpu
from jax.sharding import PartitionSpec as P

QUERY_HEADS = 16
KEY_VALUE_HEADS = 8
HEAD_SIZE = 64
CAPACITY = 80


EPSILON = 1e-06
THETA = 10000.0
MASKED = -1e30


def passed_along(value, axis, steps):
    count = lax.axis_size(axis)
    initial, last = (max(0, -steps), min(count, count - steps))
    return lax.ppermute(value, axis, [(source, source + steps) for source in range(initial, last)])


def rms_scale(values, gain):
    return values * lax.rsqrt(jnp.mean(values * values, axis=-1, keepdims=True) + EPSILON) * gain


def rotary_tables(positions, head_width):
    exponent = jnp.arange(head_width // 2, dtype=jnp.float32) * (2.0 / head_width)
    inverse = jnp.exp(-math.log(THETA) * exponent)
    angles = positions.astype(jnp.float32)[:, None] * inverse[None, :]
    return (jnp.cos(angles)[:, None, :], jnp.sin(angles)[:, None, :])


def rotate(values, cosine, sine):
    half_size = values.shape[-1] // 2
    first_half = values[..., :half_size]
    second_half = values[..., half_size:]
    return jnp.concatenate(
        [first_half * cosine - second_half * sine, second_half * cosine + first_half * sine],
        axis=-1,
    )


def rotate_back(grad_values, cosine, sine):
    half_size = grad_values.shape[-1] // 2
    first_half = grad_values[..., :half_size]
    second_half = grad_values[..., half_size:]
    return jnp.concatenate(
        [first_half * cosine + second_half * sine, second_half * cosine - first_half * sine],
        axis=-1,
    )


def head_probs(query, keys, first_row, span_len, cycle_index):
    scores = lax.dot_general(
        query, keys, (((1,), (1,)), ((), ())), preferred_element_type=jnp.float32
    ) * (HEAD_SIZE**-0.5)
    row = first_row + lax.broadcasted_iota(jnp.int32, scores.shape, 0)
    column = lax.broadcasted_iota(jnp.int32, scores.shape, 1)
    last = jnp.where(cycle_index > 0, 2 * span_len, span_len)
    allowed = (column <= row) | ((column >= span_len) & (column < last))
    scores = jnp.where(allowed, scores, MASKED)
    exps = jnp.exp(scores - jnp.max(scores, axis=-1, keepdims=True))
    return exps * (1.0 / jnp.sum(exps, axis=-1, keepdims=True))


def attend_kernel(group_size, span_len, query_ref, key_ref, value_ref, mixed_ref):
    cycle_index = lax.axis_index("blk")
    row_count, columns = query_ref.shape
    first_row = pl.program_id(0) * row_count
    for head in range(columns // HEAD_SIZE):
        here = slice(head * HEAD_SIZE, (head + 1) * HEAD_SIZE)
        copy = head // group_size
        there = slice(copy * HEAD_SIZE, (copy + 1) * HEAD_SIZE)
        probs = head_probs(query_ref[:, here], key_ref[:, there], first_row, span_len, cycle_index)
        mixed_ref[:, here] = jnp.dot(
            probs.astype(jnp.bfloat16), value_ref[:, there], preferred_element_type=jnp.float32
        ).astype(jnp.bfloat16)


def attend_back_kernel(
    group_size,
    span_len,
    query_ref,
    key_ref,
    value_ref,
    grad_ref,
    query_grad_ref,
    key_grad_ref,
    value_grad_ref,
):
    cycle_index = lax.axis_index("blk")
    row_count, columns = query_ref.shape
    first_row = pl.program_id(0) * row_count

    @pl.when(pl.program_id(0) == 0)
    def _():
        key_grad_ref[...] = jnp.zeros_like(key_grad_ref)
        value_grad_ref[...] = jnp.zeros_like(value_grad_ref)

    scale = HEAD_SIZE**-0.5
    for head in range(columns // HEAD_SIZE):
        here = slice(head * HEAD_SIZE, (head + 1) * HEAD_SIZE)
        copy = head // group_size
        there = slice(copy * HEAD_SIZE, (copy + 1) * HEAD_SIZE)
        query, grad = query_ref[:, here], grad_ref[:, here]
        keys, values = key_ref[:, there], value_ref[:, there]
        probs = head_probs(query, keys, first_row, span_len, cycle_index)
        value_grad_ref[:, there] += lax.dot_general(
            probs.astype(jnp.bfloat16),
            grad,
            (((0,), (0,)), ((), ())),
            preferred_element_type=jnp.float32,
        )
        probs_grad = lax.dot_general(
            grad, values, (((1,), (1,)), ((), ())), preferred_element_type=jnp.float32
        )
        score_grad = (
            probs * (probs_grad - jnp.sum(probs * probs_grad, axis=-1, keepdims=True))
        ).astype(jnp.bfloat16)
        query_grad_ref[:, here] = (
            jnp.dot(score_grad, keys, preferred_element_type=jnp.float32) * scale
        ).astype(jnp.bfloat16)
        key_grad_ref[:, there] += (
            lax.dot_general(
                score_grad, query, (((0,), (0,)), ((), ())), preferred_element_type=jnp.float32
            )
            * scale
        )


def attend(kernel, queries, keys, values, extra, outs, group_size, span_len):
    rows = min(queries.shape[0], max(128, 512 * 1024 // keys.shape[0]))
    row_spec = pl.BlockSpec((rows, queries.shape[1]), lambda i: (i, 0))
    key_spec = pl.BlockSpec(keys.shape, lambda i: (0, 0))
    work = queries.shape[0] * keys.shape[0] * queries.shape[1]
    return pl.pallas_call(
        functools.partial(kernel, group_size, span_len),
        grid=(queries.shape[0] // rows,),
        out_shape=outs,
        in_specs=[row_spec, key_spec, key_spec] + [row_spec] * len(extra),
        out_specs=[row_spec] + [key_spec] * (len(outs) - 1),
        compiler_params=pltpu.CompilerParams(vmem_limit_bytes=VMEM_LIMIT),
        cost_estimate=pl.CostEstimate(
            flops=4 * work, bytes_accessed=4 * 1024 * 1024, transcendentals=work // HEAD_SIZE
        ),
    )(queries, keys, values, *extra)


MESH = pl.DeviceIdType.MESH
TOKEN_AXES = ("ulysses",)
EXPERT_AXES = ("dp", "blk")
VMEM_LIMIT = 40 * 1024 * 1024


def flat_index(axes, sizes):
    index = lax.axis_index(axes[0])
    for axis, size in zip(axes[1:], sizes[1:]):
        index = index * size + lax.axis_index(axis)
    return index


def device_of(axes, sizes, index):
    place = {}
    for axis, size in zip(reversed(axes), reversed(sizes)):
        place[axis] = lax.rem(index, size)
        index = index // size
    return place


def greet(places):
    barrier = pltpu.get_barrier_semaphore()
    for place in places:
        pl.semaphore_signal(barrier, inc=1, device_id=place, device_id_type=MESH)
    pl.semaphore_wait(barrier, len(places))


def remote(source, target, send, recv, place):
    return pltpu.make_async_remote_copy(
        src_ref=source,
        dst_ref=target,
        send_sem=send,
        recv_sem=recv,
        device_id=place,
        device_id_type=MESH,
    )


def direct_copies(axes, sizes, personal, ins, outs, send, recv, local):
    count = math.prod(sizes)
    me = flat_index(axes, sizes)
    copies = []
    for step in range(1, count):
        other = lax.rem(me + step, count)
        place = device_of(axes, sizes, other)
        for item, (source, target) in enumerate(zip(ins, outs)):
            copies.append(
                remote(
                    source.at[other] if personal[item] else source,
                    target.at[me],
                    send.at[item, step],
                    recv.at[item, step],
                    place,
                )
            )
    for item, (source, target) in enumerate(zip(ins, outs)):
        copies.append(
            pltpu.make_async_copy(
                source.at[me] if personal[item] else source, target.at[me], local.at[item]
            )
        )
    return copies


def other_places(axes, sizes):
    count = math.prod(sizes)
    me = flat_index(axes, sizes)
    return [device_of(axes, sizes, lax.rem(me + step, count)) for step in range(1, count)]


def exchange_kernel(axes, sizes, personal, *refs):
    count = len(personal)
    ins, outs = refs[:count], refs[count : 2 * count]
    send, recv, local = refs[2 * count :]
    greet(other_places(axes, sizes))
    copies = direct_copies(axes, sizes, personal, ins, outs, send, recv, local)
    for copy in copies:
        copy.start()
    for copy in copies:
        copy.wait()


def exchange(values, personal, axes, sizes, collective_id):
    count = math.prod(sizes)
    shapes = [
        jax.ShapeDtypeStruct(value.shape if one else (count,) + value.shape, value.dtype)
        for value, one in zip(values, personal)
    ]
    total = len(values)
    return pl.pallas_call(
        functools.partial(exchange_kernel, axes, sizes, personal),
        out_shape=shapes,
        in_specs=[pl.BlockSpec(memory_space=pl.ANY)] * total,
        out_specs=[pl.BlockSpec(memory_space=pl.ANY)] * total,
        scratch_shapes=[
            pltpu.SemaphoreType.DMA((total, count)),
            pltpu.SemaphoreType.DMA((total, count)),
            pltpu.SemaphoreType.DMA((total,)),
        ],
        compiler_params=pltpu.CompilerParams(collective_id=collective_id, has_side_effects=True),
    )(*values)


def gather_kernel(sizes, token_sizes, wide, personal, *refs):
    near = len(personal)
    total = wide + near
    ins, outs = refs[:total], refs[total : 2 * total]
    line_send, line_recv, side_send, side_recv, local, near_send, near_recv, near_local = refs[
        2 * total :
    ]
    line, pair = sizes
    here, side = lax.axis_index("dp"), lax.axis_index("blk")
    me = here * pair + side
    across = {"blk": 1 - side}
    places = [{"dp": lax.rem(here + step, line)} for step in range(1, line)]
    greet(places + [across] + (other_places(TOKEN_AXES, token_sizes) if near else []))
    waits = []
    for item in range(wide):
        for step in range(line - 1, 0, -1):
            copy = remote(
                ins[item],
                outs[item].at[me],
                line_send.at[item, step],
                line_recv.at[item, step],
                places[step - 1],
            )
            copy.start()
        copy = remote(
            ins[item], outs[item].at[me], side_send.at[item, 0], side_recv.at[item, 0], across
        )
        copy.start()
        waits.append(copy)
        copy = pltpu.make_async_copy(ins[item], outs[item].at[me], local.at[item])
        copy.start()
        waits.append(copy)
    if near:
        for copy in direct_copies(
            TOKEN_AXES,
            token_sizes,
            personal,
            ins[wide:],
            outs[wide:],
            near_send,
            near_recv,
            near_local,
        ):
            copy.start()
            waits.append(copy)
    for step in range(1, line):
        for item in range(wide):
            arrived = remote(
                ins[item],
                outs[item].at[me],
                line_send.at[item, step],
                line_recv.at[item, step],
                places[step - 1],
            )
            arrived.wait()
            block = lax.rem(here + line - step, line) * pair + side
            copy = remote(
                outs[item].at[block],
                outs[item].at[block],
                side_send.at[item, step],
                side_recv.at[item, step],
                across,
            )
            copy.start()
            waits.append(copy)
    for copy in waits:
        copy.wait()


def gather_wide(values, near_values, personal, sizes, token_sizes, collective_id):
    count = math.prod(sizes)
    near_count = math.prod(token_sizes)
    wide, near = len(values), len(near_values)
    shapes = [jax.ShapeDtypeStruct((count,) + value.shape, value.dtype) for value in values]
    shapes += [
        jax.ShapeDtypeStruct(value.shape if one else (near_count,) + value.shape, value.dtype)
        for value, one in zip(near_values, personal)
    ]
    return pl.pallas_call(
        functools.partial(gather_kernel, sizes, token_sizes, wide, personal),
        out_shape=shapes,
        in_specs=[pl.BlockSpec(memory_space=pl.ANY)] * (wide + near),
        out_specs=[pl.BlockSpec(memory_space=pl.ANY)] * (wide + near),
        scratch_shapes=[
            pltpu.SemaphoreType.DMA((wide, sizes[0])),
            pltpu.SemaphoreType.DMA((wide, sizes[0])),
            pltpu.SemaphoreType.DMA((wide, sizes[0])),
            pltpu.SemaphoreType.DMA((wide, sizes[0])),
            pltpu.SemaphoreType.DMA((wide,)),
            pltpu.SemaphoreType.DMA((max(near, 1), near_count)),
            pltpu.SemaphoreType.DMA((max(near, 1), near_count)),
            pltpu.SemaphoreType.DMA((max(near, 1),)),
        ],
        compiler_params=pltpu.CompilerParams(collective_id=collective_id, has_side_effects=True),
    )(*values, *near_values)


def reduce_kernel(sizes, total, personal, *refs):
    small = len(personal)
    ins, refs = refs[:total], refs[total:]
    small_ins, refs = refs[:small], refs[small:]
    outs, refs = refs[:total], refs[total:]
    small_outs, refs = refs[:small], refs[small:]
    side_bufs, refs = refs[:total], refs[total:]
    sent_bufs, refs = refs[:total], refs[total:]
    line_bufs, refs = refs[:total], refs[total:]
    side_send, side_recv, line_send, line_recv, send, recv, local = refs
    line, pair = sizes
    here, side = lax.axis_index("dp"), lax.axis_index("blk")
    across = {"blk": 1 - side}
    greet(other_places(EXPERT_AXES, sizes))

    def side_copy(item, step):
        target = lax.rem(here + step, line)
        return remote(
            ins[item].at[target * pair + 1 - side],
            side_bufs[item].at[step],
            side_send.at[item, step],
            side_recv.at[item, step],
            across,
        )

    def line_copy(item, step):
        return remote(
            sent_bufs[item].at[step],
            line_bufs[item].at[step],
            line_send.at[item, step],
            line_recv.at[item, step],
            {"dp": lax.rem(here + step, line)},
        )

    order = list(range(1, line)) + [0]
    for step in order:
        for item in range(total):
            side_copy(item, step).start()
    copies = direct_copies(
        EXPERT_AXES, sizes, personal, small_ins, small_outs, send, recv, local
    )
    for copy in copies:
        copy.start()
    for step in order:
        for item in range(total):
            side_copy(item, step).wait()
            block = lax.rem(here + step, line) * pair + side
            both = ins[item][block].astype(jnp.float32) + side_bufs[item][step].astype(jnp.float32)
            if step:
                sent_bufs[item][step] = both.astype(jnp.bfloat16)
                line_copy(item, step).start()
            else:
                outs[item][...] = both
    for step in range(1, line):
        for item in range(total):
            line_copy(item, step).wait()
            outs[item][...] += line_bufs[item][step].astype(jnp.float32)
    for copy in copies:
        copy.wait()


def reduce_wide(values, small_values, personal, sizes, collective_id):
    count = math.prod(sizes)
    total, small = len(values), len(small_values)
    shapes = [jax.ShapeDtypeStruct(value.shape[1:], jnp.float32) for value in values]
    shapes += [
        jax.ShapeDtypeStruct(value.shape if one else (count,) + value.shape, value.dtype)
        for value, one in zip(small_values, personal)
    ]
    buffers = [pltpu.VMEM((sizes[0],) + value.shape[1:], jnp.bfloat16) for value in values]
    wide_sems = pltpu.SemaphoreType.DMA((total, sizes[0]))
    return pl.pallas_call(
        functools.partial(reduce_kernel, sizes, total, personal),
        out_shape=shapes,
        in_specs=[pl.BlockSpec(memory_space=pltpu.VMEM)] * (total + small),
        out_specs=[pl.BlockSpec(memory_space=pltpu.VMEM)] * (total + small),
        scratch_shapes=buffers * 3
        + [wide_sems] * 4
        + [
            pltpu.SemaphoreType.DMA((small, count)),
            pltpu.SemaphoreType.DMA((small, count)),
            pltpu.SemaphoreType.DMA((small,)),
        ],
        compiler_params=pltpu.CompilerParams(
            collective_id=collective_id, has_side_effects=True, vmem_limit_bytes=VMEM_LIMIT
        ),
    )(*values, *small_values)


def dense_gates(logits, mask):
    masked = jnp.where(mask, logits, MASKED)
    exps = jnp.where(mask, jnp.exp(masked - jnp.max(masked, axis=-1, keepdims=True)), 0.0)
    return exps / jnp.sum(exps, axis=-1, keepdims=True)


def body(
    inputs,
    gain_attn,
    query_key_value_weight,
    w_out,
    gain_mix,
    router,
    expert_in,
    expert_down,
    routes,
    cotangent,
):
    cycle_size = lax.axis_size("blk")
    slice_total = lax.axis_size("ulysses")
    sizes = (lax.axis_size("dp"), cycle_size)
    token_sizes = (slice_total,)
    groups = math.prod(sizes)
    cycle_index = lax.axis_index("blk")
    slice_index = lax.axis_index("ulysses")
    token_rows = inputs.shape[1]
    width = inputs.shape[2]
    head_width = HEAD_SIZE
    head_copies = max(1, slice_total // KEY_VALUE_HEADS)
    repeated_heads = KEY_VALUE_HEADS * head_copies
    group_size = QUERY_HEADS // repeated_heads
    local_rep = repeated_heads // slice_total
    local_query = QUERY_HEADS // slice_total
    span_len = token_rows * slice_total
    query_columns = QUERY_HEADS * head_width
    key_value_columns = KEY_VALUE_HEADS * head_width
    query_part = local_query * head_width
    pair_part = local_rep * head_width
    num_experts = router.shape[1]
    held = expert_in.shape[0]
    hidden_units = expert_down.shape[1]
    bf16 = jnp.bfloat16
    f32 = jnp.float32

    layer_in = inputs[0].astype(f32)
    norm_attn = rms_scale(layer_in, gain_attn).astype(bf16)
    mask = jnp.any(
        routes[0][:, :, None] == jnp.arange(num_experts, dtype=jnp.int32)[None, None, :], axis=1
    )
    query_start = slice_index * query_part
    pair_start = (slice_index * local_rep) // head_copies * head_width
    weight_part = jnp.concatenate(
        [
            lax.dynamic_slice_in_dim(query_key_value_weight, query_start, query_part, 1),
            lax.dynamic_slice_in_dim(
                query_key_value_weight, query_columns + pair_start, pair_part, 1
            ),
            lax.dynamic_slice_in_dim(
                query_key_value_weight,
                query_columns + key_value_columns + pair_start,
                pair_part,
                1,
            ),
            lax.dynamic_slice_in_dim(w_out, query_start, query_part, 1),
        ],
        axis=1,
    )
    first_rows = token_rows // 2
    weight_blocks, mask_blocks, first_blocks, norm_blocks = gather_wide(
        [weight_part, mask.astype(bf16).T, cotangent[0, :first_rows]],
        [norm_attn],
        (False,),
        sizes,
        token_sizes,
        0,
    )
    weights = weight_blocks.reshape(width, -1)
    own_columns = query_part + 2 * pair_part
    qkv_weight = weights[:, :own_columns]
    out_weight = weights[:, own_columns:]
    span_norm = norm_blocks.reshape(span_len, width)
    projected = jnp.dot(span_norm, qkv_weight, preferred_element_type=f32)
    span_rows = jnp.arange(span_len, dtype=jnp.int32)
    query_pos = cycle_index * span_len + span_rows
    cosine, sine = rotary_tables(query_pos, head_width)
    q_raw = projected[:, :query_part].reshape(span_len, local_query, head_width)
    key_plain = projected[:, query_part : query_part + pair_part].reshape(
        span_len, local_rep, head_width
    )
    value_plain = projected[:, query_part + pair_part :]
    queries = rotate(q_raw, cosine, sine).astype(bf16).reshape(span_len, query_part)
    own_pair = jnp.stack(
        [
            rotate(key_plain, cosine, sine).astype(bf16).reshape(span_len, pair_part),
            value_plain.astype(bf16),
        ]
    )
    earlier_pair = passed_along(own_pair, "blk", 1)
    all_keys = jnp.concatenate([own_pair[0], earlier_pair[0]], axis=0)
    all_values = jnp.concatenate([own_pair[1], earlier_pair[1]], axis=0)
    (mixed,) = attend(
        attend_kernel,
        queries,
        all_keys,
        all_values,
        [],
        [jax.ShapeDtypeStruct(queries.shape, bf16)],
        group_size,
        span_len,
    )
    branch_part = lax.dot_general(
        mixed, out_weight, (((1,), (1,)), ((), ())), preferred_element_type=f32
    )
    last_blocks, branch_blocks = gather_wide(
        [cotangent[0, first_rows:]],
        [branch_part.astype(bf16).reshape(slice_total, token_rows, width)],
        (True,),
        sizes,
        token_sizes,
        1,
    )
    residual = layer_in + jnp.sum(branch_blocks.astype(f32), axis=0)
    norm_mix = rms_scale(residual, gain_mix).astype(bf16)
    (mix_blocks,) = gather_wide([norm_mix], [], (), sizes, token_sizes, 2)

    rows = mix_blocks.reshape(groups * token_rows, width)
    row_mask = jnp.swapaxes(mask_blocks, 1, 2).reshape(groups * token_rows, num_experts) > 0
    row_gates = dense_gates(jnp.dot(rows, router, preferred_element_type=f32), row_mask)
    first_held = flat_index(EXPERT_AXES, sizes) * held
    own_gates = lax.dynamic_slice_in_dim(row_gates, first_held, held, 1)
    row_grad = (
        jnp.concatenate([first_blocks, last_blocks], axis=1)
        .reshape(groups * token_rows, width)
        .astype(f32)
    )
    combined = 0.0
    gate_grads, both_list, in_terms, down_terms = [], [], [], []
    for expert in range(held):
        weight_in, weight_down = expert_in[expert], expert_down[expert]
        gate = own_gates[:, expert : expert + 1]
        both_halves = jnp.dot(rows, weight_in, preferred_element_type=f32)
        gate_half = both_halves[:, :hidden_units]
        up_half = both_halves[:, hidden_units:]
        sigmoid_gate = jax.nn.sigmoid(gate_half)
        activated = gate_half * sigmoid_gate
        hidden = (activated * up_half).astype(bf16)
        expert_out = jnp.dot(hidden, weight_down, preferred_element_type=f32)
        combined = combined + gate * expert_out
        gate_grads.append(jnp.sum(row_grad * expert_out, axis=-1))
        expert_grad = (gate * row_grad).astype(bf16)
        hidden_grad = lax.dot_general(
            expert_grad, weight_down, (((1,), (1,)), ((), ())), preferred_element_type=f32
        )
        gate_half_grad = (
            hidden_grad * up_half * sigmoid_gate * (1.0 + gate_half * (1.0 - sigmoid_gate))
        )
        both_grad = jnp.concatenate([gate_half_grad, hidden_grad * activated], axis=-1).astype(
            bf16
        )
        both_list.append(both_grad)
        in_terms.append((rows, both_grad))
        down_terms.append((hidden, expert_grad))
    dispatch_sum = sum(
        lax.dot_general(
            both_list[expert],
            expert_in[expert],
            (((1,), (1,)), ((), ())),
            preferred_element_type=f32,
        )
        for expert in range(held)
    )

    def weight_term(pairs):
        return jnp.concatenate(
            [
                lax.dot_general(
                    left, right, (((0,), (0,)), ((), ())), preferred_element_type=f32
                ).astype(bf16)
                for left, right in pairs
            ],
            axis=0,
        )

    gate_rows = jnp.stack(gate_grads + [jnp.zeros_like(gate_grads[0])] * (-held % 8))
    gate_send = jnp.swapaxes(gate_rows.reshape(-1, groups, token_rows), 0, 1)
    in_term, combined = lax.optimization_barrier((weight_term(in_terms), combined))
    in_part = lax.psum_scatter(in_term, "ulysses", scatter_dimension=0, tiled=True)
    combined_sum, mix_grad, gate_blocks = reduce_wide(
        [
            combined.astype(bf16).reshape(groups, token_rows, width),
            dispatch_sum.astype(bf16).reshape(groups, token_rows, width),
        ],
        [gate_send],
        (True,),
        sizes,
        3,
    )
    down_terms, mix_grad = lax.optimization_barrier((down_terms, mix_grad))
    down_part = lax.psum_scatter(
        weight_term(down_terms), "ulysses", scatter_dimension=0, tiled=True
    )
    grad_expert_in = (
        lax.all_gather(in_part, "ulysses", axis=0, tiled=True)
        .astype(f32)
        .reshape(expert_in.shape)
    )
    grad_expert_down = (
        lax.all_gather(down_part, "ulysses", axis=0, tiled=True)
        .astype(f32)
        .reshape(expert_down.shape)
    )

    result = (residual + combined_sum).astype(bf16)
    out_grad = cotangent[0].astype(f32)
    gate_values = dense_gates(jnp.dot(norm_mix, router, preferred_element_type=f32), mask)
    gate_grad = gate_blocks[:, :held, :].reshape(num_experts, token_rows).T
    logit_grad = gate_values * (
        gate_grad - jnp.sum(gate_values * gate_grad, axis=-1, keepdims=True)
    )
    mix_grad = mix_grad + jnp.dot(
        logit_grad, router.astype(f32).T, precision=lax.Precision.HIGHEST
    )
    router_grad = jnp.dot(
        logit_grad.T, norm_mix.astype(f32), precision=lax.Precision.HIGHEST
    )
    _, mix_back = jax.vjp(rms_scale, residual, gain_mix)
    residual_norm_grad, gain_mix_grad = mix_back(mix_grad)
    residual_grad = out_grad + residual_norm_grad
    branch_grad = residual_grad.astype(bf16)
    shared = jnp.concatenate([router_grad, gain_mix_grad[None]], axis=0)
    shared = jnp.pad(shared, ((0, -shared.shape[0] % 8), (0, 0)))
    shared_rows = shared.shape[0]
    shared_send = jnp.swapaxes(shared.reshape(shared_rows, slice_total, -1), 0, 1)
    grad_blocks, shared_blocks = exchange(
        [branch_grad, shared_send], (False, True), TOKEN_AXES, token_sizes, 4
    )
    span_grad = grad_blocks.reshape(span_len, width)
    shared_part = jnp.sum(shared_blocks, axis=0)
    mixed_grad = jnp.dot(span_grad, out_weight, preferred_element_type=f32).astype(bf16)
    query_grad, key_grads, value_grads = attend(
        attend_back_kernel,
        queries,
        all_keys,
        all_values,
        [mixed_grad],
        [
            jax.ShapeDtypeStruct(queries.shape, bf16),
            jax.ShapeDtypeStruct(all_keys.shape, f32),
            jax.ShapeDtypeStruct(all_keys.shape, f32),
        ],
        group_size,
        span_len,
    )
    pair_grads = jnp.stack([key_grads, value_grads])
    own_grads = pair_grads[:, :span_len] + passed_along(
        pair_grads[:, span_len:].astype(bf16), "blk", -1
    ).astype(f32)
    own_grads = own_grads.astype(bf16).astype(f32)
    dq_raw = rotate_back(
        query_grad.astype(f32).reshape(span_len, local_query, head_width),
        cosine,
        sine,
    )
    dk_raw = rotate_back(own_grads[0].reshape(span_len, local_rep, head_width), cosine, sine)
    qkv_grad = jnp.concatenate(
        [
            dq_raw.reshape(span_len, query_part),
            dk_raw.reshape(span_len, pair_part),
            own_grads[1],
        ],
        axis=1,
    ).astype(bf16)
    norm_grad_part = lax.dot_general(
        qkv_grad, qkv_weight, (((1,), (1,)), ((), ())), preferred_element_type=f32
    )
    (norm_grad_blocks,) = exchange(
        [norm_grad_part.astype(bf16).reshape(slice_total, token_rows, width)],
        (True,),
        TOKEN_AXES,
        token_sizes,
        5,
    )
    attn_norm_grad = jnp.sum(norm_grad_blocks.astype(f32), axis=0)
    _, attn_back = jax.vjp(rms_scale, layer_in, gain_attn)
    input_norm_grad, gain_attn_grad = attn_back(attn_norm_grad)
    input_grad = (residual_grad + input_norm_grad).astype(bf16)
    weight_grads = jnp.concatenate(
        [
            lax.dot_general(
                span_norm, qkv_grad, (((0,), (0,)), ((), ())), preferred_element_type=f32
            ),
            lax.dot_general(
                span_grad, mixed, (((0,), (0,)), ((), ())), preferred_element_type=f32
            ),
        ],
        axis=1,
    ).astype(bf16)
    weight_sum, shared_blocks, gain_blocks = reduce_wide(
        [weight_grads.reshape(groups, width // groups, -1)],
        [shared_part, gain_attn_grad.reshape(8, -1)],
        (False, False),
        sizes,
        6,
    )
    weight_blocks, shared_blocks, gain_blocks = exchange(
        [
            weight_sum.astype(bf16),
            jnp.sum(shared_blocks, axis=0),
            jnp.sum(gain_blocks, axis=0),
        ],
        (False, False, False),
        TOKEN_AXES,
        token_sizes,
        7,
    )
    weight_blocks = weight_blocks.astype(f32)

    def columns(first, count, copies):
        part = weight_blocks[:, :, first : first + count]
        part = part.reshape(slice_total // copies, copies, part.shape[1], count)
        return jnp.swapaxes(jnp.sum(part, axis=1), 0, 1).reshape(part.shape[2], -1)

    grad_w_qkv = jnp.concatenate(
        [
            columns(0, query_part, 1),
            columns(query_part, pair_part, head_copies),
            columns(query_part + pair_part, pair_part, head_copies),
        ],
        axis=1,
    )
    grad_w_out = columns(own_columns, query_part, 1)
    shared_sum = jnp.swapaxes(shared_blocks, 0, 1).reshape(shared_rows, width)
    return (
        result[None],
        input_grad[None],
        jnp.sum(gain_blocks, axis=0).reshape(width),
        grad_w_qkv,
        grad_w_out,
        shared_sum[num_experts],
        shared_sum[:num_experts].T,
        grad_expert_in,
        grad_expert_down,
    )


def solution(mesh):
    in_specs = (
        P("dp", ("blk", "ulysses"), None),
        P(),
        P(("dp", "blk"), None),
        P(("dp", "blk"), None),
        P(),
        P(),
        P(("dp", "blk"), None, None),
        P(("dp", "blk"), None, None),
        P("dp", ("blk", "ulysses"), None),
        P("dp", ("blk", "ulysses"), None),
    )
    out_specs = (
        P("dp", ("blk", "ulysses"), None),
        P("dp", ("blk", "ulysses"), None),
        P(),
        P(("dp", "blk"), None),
        P(("dp", "blk"), None),
        P(),
        P(),
        P(("dp", "blk"), None, None),
        P(("dp", "blk"), None, None),
    )
    return jax.shard_map(body, mesh=mesh, in_specs=in_specs, out_specs=out_specs, check_vma=False)
```
